32 devices in a mesh: slices: 2 (over y), scan: 4 (over z), band: 2 (over x), pix: 2 (over core).
Axes of the slice: x: 2, y: 2, z: 4, core: 2. Of those that a mesh axis runs over, the one named last changes fastest.
Arguments:
- frames: bfloat16 [1024, 524288], P(('slices', 'scan'), ('band', 'pix')), parts along dimension 0, may hold values from -6 to 6
- pixel_weight: bfloat16 [524288], P(('band', 'pix')), may hold values from 0.29882812 to 3
- pixel_slot: int32 [524288], P(('band', 'pix')), may hold values from 0 to 127
- block_tile: int32 [4096], P(('band', 'pix')), may hold values from 0 to 15
- spectra: float32 [64, 2048], P(None, ('scan', 'band', 'pix')), may hold values from 0.1 to 1
- ray_index: int32 [4, 512, 512], P(None, ('scan', 'pix')), may hold values from 0 to 127, as said below
Outputs:
- images: float32 [128, 512, 512], P(('slices', 'band'), ('scan', 'pix')), parts along dimension 0
The draws below stay inside these ranges and needn't reach their ends.
There are 2 independent parts, one for each index of `slices`. The reference program is written for one: setup_inputs(seed, part) draws one part's arguments, and reference() takes and returns one part's arrays. A program takes and returns all parts, laid end to end along the dimension named above; an argument that names none is the same for every part. Nothing has to cross between parts.
Inputs may be any that keep to these rules, and one draw needn't show every extreme that they name: `ray_index`: every translation index is met by at least one image pixel at every angle.
All inputs are finite; a program needn't handle non-finite values.
Results may differ from the reference program's by a relative error of at most 0.0003.
Values sent between devices are 32-bit elements; how exact they have to be, the bound alone decides.
A program may use at most 320 MiB of HBM per device.

```python
import math
import jax
import jax.numpy as jnp
from jax import lax

NA = 4
NT = 128
PIX = 524288
TILE = 128
Q = 2048
C = 64
IMG = 512
ITERS = 3
POS = 512


def draw_ray_index(key, part):
    key = jax.random.fold_in(key, 7)
    first_key, second_key = jax.random.split(key)
    step_row = jax.random.randint(first_key, (NA, 1, 1), 1, 9)
    step_col = jax.random.randint(second_key, (NA, 1, 1), -8, 9)
    row_index = jnp.arange(IMG, dtype=jnp.int32)[None, :, None]
    col_index = jnp.arange(IMG, dtype=jnp.int32)[None, None, :]
    offset = row_index * step_row + col_index * step_col - jnp.minimum(step_col, 0) * (IMG - 1)
    spread = (IMG - 1) * (step_row + jnp.abs(step_col)) + 1
    return (offset * NT // spread).astype(jnp.int32)


def plant(entries, rng, least, high):
    longest = entries.shape.index(max(entries.shape))
    spots = []
    for shift in (0, 1):
        where = [jax.random.randint(jax.random.fold_in(rng, axis), (), 0, length) for axis, length in enumerate(entries.shape)]
        where[longest] = (where[longest] + shift) % entries.shape[longest]
        spots.append(tuple(where))
    return entries.at[spots[0]].set(least).at[spots[1]].set(high)


def block_levels(stream_key, shape, cuts, smallest, high):
    level, own = 1.0, jax.random.fold_in(stream_key, 6)
    for dim, shards_of in cuts:
        draws = jnp.exp(jax.random.uniform(jax.random.fold_in(own, dim), (shards_of,), jnp.float32, smallest / len(cuts), high / len(cuts)))
        level = level * jnp.repeat(draws, shape[dim] // shards_of).reshape([-1 if axis == dim else 1 for axis in range(len(shape))])
    return level


def normal_values(stream_key, dims, scale, limit, shards=(), held_as=jnp.bfloat16):
    array = scale * jax.random.normal(stream_key, dims, jnp.float32)
    if shards:
        array = array * block_levels(stream_key, dims, shards, -0.22, 0.18)
    return jnp.clip(array, -limit, limit).astype(held_as)


def setup_inputs(seed: int = 0, part: int = 0) -> dict:
    keys = jax.random.split(jax.random.key(seed), 7)
    part_splits = jax.random.split(jax.random.fold_in(keys[6], part), 7)
    return {
        "frames": normal_values(part_splits[0], (POS, PIX), 1.0, 6.0, ((0, 4), (1, 4))),
        "pixel_weight": jnp.clip(jnp.exp(math.log(3.0) - 2.306499 * jax.random.uniform(keys[1], (PIX,), jnp.float32) ** block_levels(keys[1], (PIX,), ((0, 4),), -0.2, 0.2)), 0.29882812, 3.0).astype(jnp.bfloat16),
        "pixel_slot": plant(jax.random.randint(keys[2], (PIX,), 0, TILE), jax.random.fold_in(keys[2], 1), 0, TILE - 1).astype(jnp.int32),
        "block_tile": plant(jax.random.randint(keys[3], (PIX // TILE,), 0, Q // TILE), jax.random.fold_in(keys[3], 1), 0, (Q // TILE) - 1).astype(jnp.int32),
        "spectra": jnp.clip(jnp.exp(math.log(1.0) - 2.3025851 * jax.random.uniform(keys[4], (C, Q), jnp.float32) ** block_levels(keys[4], (C, Q), ((1, 16),), -0.2, 0.2)), 0.1, 1.0),
        "ray_index": draw_ray_index(jax.random.fold_in(keys[6], 71), part),
    }


RELAX = 1.5

def reference(frames, pixel_weight, pixel_slot, block_tile, spectra, ray_index):
    highest = lax.Precision.HIGHEST
    bins_all = (jnp.repeat(block_tile, TILE) * TILE + pixel_slot).astype(jnp.int32)
    piece_len = PIX // 8

    def accumulate(block_index, running):
        offset = (block_index * piece_len).astype(jnp.int32)
        weighted = lax.dynamic_slice_in_dim(frames, offset, piece_len, 1).astype(jnp.float32)
        weighted = weighted * lax.dynamic_slice_in_dim(pixel_weight, offset, piece_len, 0).astype(jnp.float32)[None, :]
        labels = lax.dynamic_slice_in_dim(bins_all, offset, piece_len, 0)
        return running + jax.ops.segment_sum(weighted.T, labels, num_segments=Q)
    summed = lax.fori_loop(0, 8, accumulate, jnp.zeros((Q, POS), jnp.float32))
    integrated = summed.T
    gram_total = jnp.dot(spectra, spectra.T, precision=highest)
    moments = jnp.dot(integrated, spectra.T, precision=highest)
    factor = jnp.linalg.cholesky(gram_total)
    coefficients = jax.scipy.linalg.cho_solve((factor, True), moments.T).T
    ray_flat = ray_index.reshape(NA, IMG * IMG)
    ones_row = jnp.ones((IMG * IMG,), jnp.float32)
    ray_count = jax.vmap(lambda labels: jax.ops.segment_sum(ones_row, labels, num_segments=NT))(ray_flat).reshape(POS)
    images = jnp.zeros((C, IMG * IMG), jnp.float32)
    for sweep in range(ITERS):
        if sweep == 0:
            residual = coefficients
        else:
            current = images.T
            projected = jax.vmap(lambda labels: jax.ops.segment_sum(current, labels, num_segments=NT))(ray_flat)
            residual = coefficients - projected.reshape(POS, C) / IMG
        weighted_res = (residual / ray_count[:, None]).reshape(NA, NT, C)
        backward = jnp.zeros((IMG * IMG, C), jnp.float32)
        for angle_index in range(NA):
            backward = backward + weighted_res[angle_index][ray_flat[angle_index]]
        images = images + RELAX * IMG / NA * backward.T
    return images.reshape(C, IMG, IMG)
```

```python
import functools

import jax
import jax.numpy as jnp
from jax import lax
from jax.experimental import pallas as pl
from jax.experimental.pallas import tpu as pltpu
from jax.sharding import PartitionSpec as P

TILE = 128
Q = 2048
ITERS = 3
RELAX = 1.5
CHUNK = 8192
NT_DIMS = (((1,), (1,)), ((), ()))


def bin_kernel(tile_ref, frames_ref, slot_ref, weight_ref, out_ref, *, blocks):
    step = pl.program_id(0)
    pos = frames_ref.shape[0]

    @pl.when(step == 0)
    def _():
        out_ref[...] = jnp.zeros_like(out_ref)

    row_id = lax.broadcasted_iota(jnp.int32, (TILE, TILE), 0).astype(jnp.bfloat16)
    zero = jnp.zeros((TILE, TILE), jnp.bfloat16)
    for pair in range(blocks // 2):
        parts = []
        for half in range(2):
            b = 2 * pair + half
            slot = jnp.broadcast_to(slot_ref[b : b + 1, :].astype(jnp.float32), (TILE, TILE))
            weight = jnp.broadcast_to(weight_ref[b : b + 1, :].astype(jnp.float32), (TILE, TILE))
            spread = jnp.where(slot.astype(jnp.bfloat16) == row_id, weight.astype(jnp.bfloat16), zero)
            parts.append(
                jnp.concatenate([spread, zero] if half == 0 else [zero, spread], axis=1)
            )
        spread = jnp.concatenate(parts, axis=0)
        both = lax.dot_general(
            frames_ref[:, 2 * pair * TILE : (2 * pair + 2) * TILE],
            spread,
            NT_DIMS,
            preferred_element_type=jnp.float32,
        )
        for half in range(2):
            t = tile_ref[step * blocks + 2 * pair + half]
            out_ref[t] += both[:, half * TILE : (half + 1) * TILE]


def bin_frames(frames, pixel_weight, pixel_slot, block_tile):
    pos, pixels = frames.shape
    chunk = min(CHUNK, pixels)
    blocks = chunk // TILE
    tiles = Q // TILE
    return pl.pallas_call(
        functools.partial(bin_kernel, blocks=blocks),
        grid_spec=pltpu.PrefetchScalarGridSpec(
            num_scalar_prefetch=1,
            grid=(pixels // chunk,),
            in_specs=[
                pl.BlockSpec((pos, chunk), lambda i, t: (0, i)),
                pl.BlockSpec((blocks, TILE), lambda i, t: (i, 0)),
                pl.BlockSpec((blocks, TILE), lambda i, t: (i, 0)),
            ],
            out_specs=pl.BlockSpec((tiles, pos, TILE), lambda i, t: (0, 0, 0)),
        ),
        out_shape=jax.ShapeDtypeStruct((tiles, pos, TILE), jnp.float32),
        compiler_params=pltpu.CompilerParams(vmem_limit_bytes=40 * 1024 * 1024),
        cost_estimate=pl.CostEstimate(
            flops=4 * pos * pixels * TILE, bytes_accessed=2 * pos * pixels, transcendentals=0
        ),
        name="bin_frames",
    )(
        block_tile,
        frames,
        pixel_slot.reshape(-1, TILE),
        pixel_weight.reshape(-1, TILE),
    )


def pair_kernel(ray_ref, out_ref, *, translations):
    angles, rows, width = ray_ref.shape
    row_id = lax.broadcasted_iota(jnp.int32, (translations, width), 0).astype(jnp.bfloat16)
    one = jnp.ones((translations, width), jnp.bfloat16)
    zero = jnp.zeros((translations, width), jnp.bfloat16)
    out_ref[...] = jnp.zeros_like(out_ref)
    for r in range(rows):
        hits = []
        for a in range(angles):
            index = jnp.broadcast_to(
                ray_ref[a, r : r + 1, :].astype(jnp.float32), (translations, width)
            ).astype(jnp.bfloat16)
            hits.append(jnp.where(index == row_id, one, zero))
        hits = jnp.concatenate(hits, axis=0)
        out_ref[...] += lax.dot_general(hits, hits, NT_DIMS, preferred_element_type=jnp.float32)


def pair_counts(rays, translations):
    angles, rows, width = rays.shape
    total = angles * translations
    return pl.pallas_call(
        functools.partial(pair_kernel, translations=translations),
        out_shape=jax.ShapeDtypeStruct((total, total), jnp.float32),
        compiler_params=pltpu.CompilerParams(vmem_limit_bytes=40 * 1024 * 1024),
        cost_estimate=pl.CostEstimate(
            flops=2 * total * total * rows * width, bytes_accessed=4 * total * total, transcendentals=0
        ),
        name="pair_counts",
    )(rays)


def back_kernel(table_ref, ray_ref, out_ref, *, translations):
    comps, rows, width = out_ref.shape
    angles = ray_ref.shape[0]

    def one_comp(c, carry):
        rows_of = table_ref[c]
        tables = [jnp.broadcast_to(rows_of[a : a + 1, :], (8, translations)) for a in range(angles)]
        for r in range(0, rows, 8):
            for w in range(0, width, translations):
                value = None
                for a in range(angles):
                    index = ray_ref[a, r : r + 8, w : w + translations]
                    got = jnp.take_along_axis(
                        tables[a], index, axis=1, mode="promise_in_bounds"
                    )
                    value = got if value is None else value + got
                out_ref[c, r : r + 8, w : w + translations] = value
        return carry

    lax.fori_loop(0, comps, one_comp, 0)


def back_project(table, rays, translations):
    comps = table.shape[0]
    angles, rows, width = rays.shape
    group = min(8, comps)
    return pl.pallas_call(
        functools.partial(back_kernel, translations=translations),
        grid=(comps // group,),
        in_specs=[
            pl.BlockSpec((group, angles, translations), lambda i: (i, 0, 0)),
            pl.BlockSpec((angles, rows, width), lambda i: (0, 0, 0)),
        ],
        out_specs=pl.BlockSpec((group, rows, width), lambda i: (i, 0, 0)),
        out_shape=jax.ShapeDtypeStruct((comps, rows, width), jnp.float32),
        compiler_params=pltpu.CompilerParams(vmem_limit_bytes=40 * 1024 * 1024),
        cost_estimate=pl.CostEstimate(
            flops=comps * angles * rows * width, bytes_accessed=4 * comps * rows * width, transcendentals=0
        ),
        name="back_project",
    )(table.reshape(comps, angles, translations), rays)


def shards(frames, pixel_weight, pixel_slot, block_tile, spectra, ray_index):
    highest = lax.Precision.HIGHEST
    scan_count = lax.axis_size("scan")
    band_count = lax.axis_size("band")
    pos_local, pix_local = frames.shape
    comp_total, bin_local = spectra.shape
    angles, row_local, img_width = ray_index.shape
    pos_total = pos_local * scan_count
    translations = pos_total // angles
    comp_local = comp_total // band_count
    first_comp = lax.axis_index("band") * comp_local

    copies = lax.axis_size("slices") * band_count
    copy_id = lax.axis_index("slices") * band_count + lax.axis_index("band")
    share = row_local // copies
    own_rays = lax.dynamic_slice_in_dim(ray_index, copy_id * share, share, 1)
    counts = lax.psum(pair_counts(own_rays, translations), ("slices", "scan", "band", "pix"))
    all_spectra = lax.all_gather(spectra, ("scan", "band", "pix"), axis=1, tiled=True)

    bins = bin_frames(frames, pixel_weight, pixel_slot, block_tile)

    gram = lax.dot_general(all_spectra, all_spectra, NT_DIMS, precision=highest)
    factor = jnp.linalg.cholesky(gram)
    moments_part = jnp.einsum(
        "ctl,tpl->cp", all_spectra.reshape(comp_total, Q // TILE, TILE), bins, precision=highest
    )
    place = lax.axis_index("scan") * pos_local
    moments_wide = lax.dynamic_update_slice_in_dim(
        jnp.zeros((comp_total, pos_total), jnp.float32), moments_part, place, 1
    )
    moments = lax.psum(moments_wide, ("scan", "band", "pix"))
    all_coefficients = jax.scipy.linalg.cho_solve((factor, True), moments)
    coefficients = lax.dynamic_slice_in_dim(all_coefficients, first_comp, comp_local, 0)
    ray_count = jnp.diagonal(counts)[None, :]
    total = jnp.zeros((comp_local, pos_total), jnp.float32)
    for sweep in range(ITERS):
        residual = coefficients
        if sweep > 0:
            residual = coefficients - (RELAX / angles) * jnp.dot(total, counts, precision=highest)
        total = total + residual / ray_count
    return back_project((RELAX * img_width / angles) * total, ray_index, translations)


def solution(mesh):
    return jax.shard_map(
        shards,
        mesh=mesh,
        in_specs=(
            P(("slices", "scan"), ("band", "pix")),
            P(("band", "pix")),
            P(("band", "pix")),
            P(("band", "pix")),
            P(None, ("scan", "band", "pix")),
            P(None, ("scan", "pix"), None),
        ),
        out_specs=P(("slices", "band"), ("scan", "pix"), None),
        check_vma=False,
    )
```

```python
import functools

import jax
import jax.numpy as jnp
from jax import lax
from jax.experimental import pallas as pl
from jax.experimental.pallas import tpu as pltpu
from jax.sharding import PartitionSpec as P

TILE = 128
Q = 2048
ITERS = 3
RELAX = 1.5
CHUNK = 8192
MESH = pl.DeviceIdType.MESH
NT_DIMS = (((1,), (1,)), ((), ()))


def bin_kernel(tile_ref, frames_ref, slot_ref, weight_ref, out_ref, *, blocks):
    step = pl.program_id(0)
    pos = frames_ref.shape[0]

    @pl.when(step == 0)
    def _():
        out_ref[...] = jnp.zeros_like(out_ref)

    row_id = lax.broadcasted_iota(jnp.int32, (TILE, TILE), 0).astype(jnp.bfloat16)
    zero = jnp.zeros((TILE, TILE), jnp.bfloat16)
    for pair in range(blocks // 2):
        parts = []
        for half in range(2):
            b = 2 * pair + half
            slot = jnp.broadcast_to(slot_ref[b : b + 1, :].astype(jnp.float32), (TILE, TILE))
            weight = jnp.broadcast_to(weight_ref[b : b + 1, :].astype(jnp.float32), (TILE, TILE))
            spread = jnp.where(slot.astype(jnp.bfloat16) == row_id, weight.astype(jnp.bfloat16), zero)
            parts.append(
                jnp.concatenate([spread, zero] if half == 0 else [zero, spread], axis=1)
            )
        spread = jnp.concatenate(parts, axis=0)
        both = lax.dot_general(
            frames_ref[:, 2 * pair * TILE : (2 * pair + 2) * TILE],
            spread,
            NT_DIMS,
            preferred_element_type=jnp.float32,
        )
        for half in range(2):
            t = tile_ref[step * blocks + 2 * pair + half]
            out_ref[t] += both[:, half * TILE : (half + 1) * TILE]


def bin_frames(frames, pixel_weight, pixel_slot, block_tile):
    pos, pixels = frames.shape
    chunk = min(CHUNK, pixels)
    blocks = chunk // TILE
    tiles = Q // TILE
    return pl.pallas_call(
        functools.partial(bin_kernel, blocks=blocks),
        grid_spec=pltpu.PrefetchScalarGridSpec(
            num_scalar_prefetch=1,
            grid=(pixels // chunk,),
            in_specs=[
                pl.BlockSpec((pos, chunk), lambda i, t: (0, i)),
                pl.BlockSpec((blocks, TILE), lambda i, t: (i, 0)),
                pl.BlockSpec((blocks, TILE), lambda i, t: (i, 0)),
            ],
            out_specs=pl.BlockSpec((tiles, pos, TILE), lambda i, t: (0, 0, 0)),
        ),
        out_shape=jax.ShapeDtypeStruct((tiles, pos, TILE), jnp.float32),
        compiler_params=pltpu.CompilerParams(vmem_limit_bytes=40 * 1024 * 1024),
        cost_estimate=pl.CostEstimate(
            flops=4 * pos * pixels * TILE, bytes_accessed=2 * pos * pixels, transcendentals=0
        ),
        name="bin_frames",
    )(
        block_tile,
        frames,
        pixel_slot.reshape(-1, TILE),
        pixel_weight.reshape(-1, TILE),
    )


def pair_kernel(ray_ref, out_ref, count_ref):
    step = pl.program_id(0)
    angles, rows, width = ray_ref.shape
    nt = out_ref.shape[0] // angles
    row_id = lax.broadcasted_iota(jnp.int32, (nt, width), 0).astype(jnp.bfloat16)
    one = jnp.ones((nt, width), jnp.bfloat16)
    zero = jnp.zeros((nt, width), jnp.bfloat16)

    @pl.when(step == 0)
    def _():
        out_ref[...] = jnp.zeros_like(out_ref)

    def meet(left, right):
        return lax.dot_general(left, right, NT_DIMS, preferred_element_type=jnp.float32)

    for r in range(rows):
        hits = []
        for a in range(angles):
            index = jnp.broadcast_to(ray_ref[a, r : r + 1, :].astype(jnp.float32), (nt, width))
            hits.append(jnp.where(index.astype(jnp.bfloat16) == row_id, one, zero))
        first = jnp.concatenate(hits[:2], axis=0)
        last = jnp.concatenate(hits[2:], axis=0)
        out_ref[: 2 * nt, 2 * nt :] += meet(first, last)
        out_ref[:nt, : 2 * nt] += meet(hits[0], first)
        out_ref[2 * nt : 3 * nt, 2 * nt :] += meet(hits[2], last)

    @pl.when(step == pl.num_programs(0) - 1)
    def _():
        same = lax.broadcasted_iota(jnp.int32, (nt, nt), 0) == lax.broadcasted_iota(jnp.int32, (nt, nt), 1)
        for base in (0, 2 * nt):
            block = out_ref[base : base + nt, base : base + 2 * nt]
            held = jnp.sum(block, axis=0, keepdims=True)
            count_ref[:, base : base + 2 * nt] = jnp.broadcast_to(held, (8, 2 * nt))
            out_ref[base + nt : base + 2 * nt, base : base + nt] = block[:, nt:].T
            out_ref[base + nt : base + 2 * nt, base + nt : base + 2 * nt] = jnp.where(
                same, jnp.broadcast_to(held[:, nt:], (nt, nt)), 0.0
            )
        out_ref[2 * nt :, : 2 * nt] = out_ref[: 2 * nt, 2 * nt :].T


def pair_counts(rays, translations):
    angles, rows, width = rays.shape
    total = angles * translations
    return pl.pallas_call(
        pair_kernel,
        grid=(rows // 8,),
        in_specs=[pl.BlockSpec((angles, 8, width), lambda i: (0, i, 0))],
        out_specs=[
            pl.BlockSpec((total, total), lambda i: (0, 0)),
            pl.BlockSpec((8, total), lambda i: (0, 0)),
        ],
        out_shape=[
            jax.ShapeDtypeStruct((total, total), jnp.float32),
            jax.ShapeDtypeStruct((8, total), jnp.float32),
        ],
        compiler_params=pltpu.CompilerParams(vmem_limit_bytes=40 * 1024 * 1024),
        cost_estimate=pl.CostEstimate(
            flops=total * total * rows * width, bytes_accessed=4 * total * total, transcendentals=0
        ),
        name="pair_counts",
    )(rays)


def greet(peers):
    barrier = pltpu.get_barrier_semaphore()
    for peer in peers:
        pl.semaphore_signal(barrier, inc=1, device_id=peer, device_id_type=MESH)
    pl.semaphore_wait(barrier, len(peers))


def others(axis, size):
    me = lax.axis_index(axis)
    return [{axis: lax.rem(me + d, size)} for d in range(1, size)]


def swap(axis, size, send, land, send_sem, recv_sem):
    me = lax.axis_index(axis)
    copies = [
        pltpu.make_async_remote_copy(
            src_ref=send,
            dst_ref=land(me),
            send_sem=send_sem.at[d],
            recv_sem=recv_sem.at[d],
            device_id={axis: lax.rem(me + d, size)},
            device_id_type=MESH,
        )
        for d in range(1, size)
    ]
    for copy in copies:
        copy.start()
    return copies


def gather_kernel(own_ref, all_ref, send_sem, recv_sem, *, scan, band, pix):
    s, b, p = lax.axis_index("scan"), lax.axis_index("band"), lax.axis_index("pix")
    greet(others("scan", scan) + others("band", band) + others("pix", pix))
    all_ref[p, b, s] = own_ref[...]
    for copy in swap(
        "scan", scan, all_ref.at[p, b, s], lambda r: all_ref.at[p, b, r], send_sem.at[0], recv_sem.at[0]
    ):
        copy.wait()
    for copy in swap(
        "band", band, all_ref.at[p, b], lambda r: all_ref.at[p, r], send_sem.at[1], recv_sem.at[1]
    ):
        copy.wait()
    for copy in swap("pix", pix, all_ref.at[p], lambda r: all_ref.at[r], send_sem.at[2], recv_sem.at[2]):
        copy.wait()


def gather_spectra(spectra, scan, band, pix):
    comps, width = spectra.shape
    most = max(scan, band, pix)
    whole = pl.pallas_call(
        functools.partial(gather_kernel, scan=scan, band=band, pix=pix),
        out_shape=jax.ShapeDtypeStruct((pix, band, scan, comps, width), jnp.float32),
        in_specs=[pl.BlockSpec(memory_space=pltpu.VMEM)],
        out_specs=pl.BlockSpec(memory_space=pltpu.VMEM),
        scratch_shapes=[pltpu.SemaphoreType.DMA((3, most)), pltpu.SemaphoreType.DMA((3, most))],
        compiler_params=pltpu.CompilerParams(
            collective_id=0, has_side_effects=True, vmem_limit_bytes=40 * 1024 * 1024
        ),
        name="gather_spectra",
    )(spectra)
    return whole.transpose(3, 2, 1, 0, 4).reshape(comps, scan * band * pix * width)


def sirt_kernel(
    part_ref, pairs_ref, count_ref, out_ref,
    group, place, count_pix, count_mid, count_scan, proj, proj_pix, proj_mid, proj_scan,
    send_sem, recv_sem, *, scan, band, pix, scale,
):
    s, b, p = lax.axis_index("scan"), lax.axis_index("band"), lax.axis_index("pix")
    sizes = band * pix
    rank = b * pix + p
    group_peers = []
    for d in range(1, sizes):
        peer = lax.rem(rank + d, sizes)
        group_peers.append({"band": lax.div(peer, pix), "pix": lax.rem(peer, pix)})
    greet(group_peers + others("scan", scan))

    copies = []
    for d, peer in zip(range(1, sizes), group_peers):
        copy = pltpu.make_async_remote_copy(
            src_ref=part_ref.at[peer["band"]],
            dst_ref=group.at[d],
            send_sem=send_sem.at[0, d],
            recv_sem=recv_sem.at[0, d],
            device_id=peer,
            device_id_type=MESH,
        )
        copy.start()
        copies.append(copy)
    copies += swap("pix", pix, count_ref, lambda r: count_pix.at[r], send_sem.at[1], recv_sem.at[1])
    count_pix[p] = count_ref[...]
    for copy in copies:
        copy.wait()
    value = part_ref[b]
    for d in range(1, sizes):
        value += group[d]
    place[s] = value
    counted = count_pix[0]
    for r in range(1, pix):
        counted += count_pix[r]
    count_mid[...] = counted
    count_scan[s] = counted
    copies = swap("scan", scan, place.at[s], lambda r: place.at[r], send_sem.at[2], recv_sem.at[2])
    copies += swap("scan", scan, count_mid, lambda r: count_scan.at[r], send_sem.at[3], recv_sem.at[3])
    for copy in copies:
        copy.wait()
    counted = count_scan[0]
    for r in range(1, scan):
        counted += count_scan[r]
    coefficients = jnp.concatenate([place[r] for r in range(scan)], axis=1)
    comps, rays = coefficients.shape
    ray_count = jnp.broadcast_to(counted[0:1], (comps, rays))
    total = coefficients / ray_count
    for k in range(ITERS - 1):
        local = lax.dot_general(
            total, pairs_ref[...], (((1,), (0,)), ((), ())),
            precision=lax.Precision.HIGHEST, preferred_element_type=jnp.float32,
        )
        proj[k] = local
        proj_pix[k, p] = local
        for copy in swap(
            "pix", pix, proj.at[k], lambda r: proj_pix.at[k, r], send_sem.at[4 + 2 * k], recv_sem.at[4 + 2 * k]
        ):
            copy.wait()
        value = proj_pix[k, 0]
        for r in range(1, pix):
            value += proj_pix[k, r]
        proj_mid[k] = value
        proj_scan[k, s] = value
        for copy in swap(
            "scan", scan, proj_mid.at[k], lambda r: proj_scan.at[k, r], send_sem.at[5 + 2 * k], recv_sem.at[5 + 2 * k]
        ):
            copy.wait()
        value = proj_scan[k, 0]
        for r in range(1, scan):
            value += proj_scan[k, r]
        total += (coefficients - scale * value) / ray_count
    out_ref[...] = total


def sirt_table(parts, pairs, counts, scan, pix, scale):
    band, comps, pos = parts.shape
    rays = pairs.shape[0]
    most = max(scan, band * pix)
    steps = ITERS - 1
    vmem = pl.BlockSpec(memory_space=pltpu.VMEM)
    f32 = jnp.float32
    return pl.pallas_call(
        functools.partial(sirt_kernel, scan=scan, band=band, pix=pix, scale=scale),
        out_shape=jax.ShapeDtypeStruct((comps, rays), f32),
        in_specs=[vmem] * 3,
        out_specs=vmem,
        scratch_shapes=[
            pltpu.VMEM((band * pix, comps, pos), f32),
            pltpu.VMEM((scan, comps, pos), f32),
            pltpu.VMEM((pix, 8, rays), f32),
            pltpu.VMEM((8, rays), f32),
            pltpu.VMEM((scan, 8, rays), f32),
            pltpu.VMEM((steps, comps, rays), f32),
            pltpu.VMEM((steps, pix, comps, rays), f32),
            pltpu.VMEM((steps, comps, rays), f32),
            pltpu.VMEM((steps, scan, comps, rays), f32),
            pltpu.SemaphoreType.DMA((4 + 2 * steps, most)),
            pltpu.SemaphoreType.DMA((4 + 2 * steps, most)),
        ],
        compiler_params=pltpu.CompilerParams(
            collective_id=1, has_side_effects=True, vmem_limit_bytes=40 * 1024 * 1024
        ),
        name="sirt_table",
    )(parts, pairs, counts)


def back_kernel(table_ref, ray_ref, out_ref, *, translations):
    comps, rows, width = out_ref.shape
    angles = ray_ref.shape[0]

    def one_comp(c, carry):
        rows_of = table_ref[c]
        tables = [jnp.broadcast_to(rows_of[a : a + 1, :], (8, translations)) for a in range(angles)]
        for r in range(0, rows, 8):
            for w in range(0, width, translations):
                value = None
                for a in range(angles):
                    index = ray_ref[a, r : r + 8, w : w + translations]
                    got = jnp.take_along_axis(
                        tables[a], index, axis=1, mode="promise_in_bounds"
                    )
                    value = got if value is None else value + got
                out_ref[c, r : r + 8, w : w + translations] = value
        return carry

    lax.fori_loop(0, comps, one_comp, 0)


def back_project(table, rays, translations):
    comps = table.shape[0]
    angles, rows, width = rays.shape
    group = min(8, comps)
    return pl.pallas_call(
        functools.partial(back_kernel, translations=translations),
        grid=(comps // group,),
        in_specs=[
            pl.BlockSpec((group, angles, translations), lambda i: (i, 0, 0)),
            pl.BlockSpec((angles, rows, width), lambda i: (0, 0, 0)),
        ],
        out_specs=pl.BlockSpec((group, rows, width), lambda i: (i, 0, 0)),
        out_shape=jax.ShapeDtypeStruct((comps, rows, width), jnp.float32),
        compiler_params=pltpu.CompilerParams(vmem_limit_bytes=40 * 1024 * 1024),
        cost_estimate=pl.CostEstimate(
            flops=comps * angles * rows * width, bytes_accessed=4 * comps * rows * width, transcendentals=0
        ),
        name="back_project",
    )(table.reshape(comps, angles, translations), rays)


def shards(frames, pixel_weight, pixel_slot, block_tile, spectra, ray_index):
    highest = lax.Precision.HIGHEST
    scan_count = lax.axis_size("scan")
    band_count = lax.axis_size("band")
    pos_local, pix_local = frames.shape
    comp_total, bin_local = spectra.shape
    angles, row_local, img_width = ray_index.shape
    pos_total = pos_local * scan_count
    translations = pos_total // angles
    comp_local = comp_total // band_count

    pix_count = lax.axis_size("pix")
    all_spectra = gather_spectra(spectra, scan_count, band_count, pix_count)
    pairs, counts = pair_counts(ray_index, translations)
    bins = bin_frames(frames, pixel_weight, pixel_slot, block_tile)
    gram = lax.dot_general(all_spectra, all_spectra, NT_DIMS, precision=highest)
    factor = jnp.linalg.cholesky(gram)
    moments_part = jnp.einsum(
        "ctl,tpl->cp", all_spectra.reshape(comp_total, Q // TILE, TILE), bins, precision=highest
    )
    parts = jax.scipy.linalg.cho_solve((factor, True), moments_part)
    parts = parts.reshape(band_count, comp_local, pos_local)
    total = sirt_table(parts, pairs, counts, scan_count, pix_count, RELAX / angles)
    return back_project((RELAX * img_width / angles) * total, ray_index, translations)


def solution(mesh):
    return jax.shard_map(
        shards,
        mesh=mesh,
        in_specs=(
            P(("slices", "scan"), ("band", "pix")),
            P(("band", "pix")),
            P(("band", "pix")),
            P(("band", "pix")),
            P(None, ("scan", "band", "pix")),
            P(None, ("scan", "pix"), None),
        ),
        out_specs=P(("slices", "band"), ("scan", "pix"), None),
        check_vma=False,
    )
```

```python
import functools

import jax
import jax.numpy as jnp
from jax import lax
from jax.experimental import pallas as pl
from jax.experimental.pallas import tpu as pltpu
from jax.sharding import PartitionSpec as P

TILE = 128
Q = 2048
ITERS = 3
RELAX = 1.5
CHUNK = 8192
MESH = pl.DeviceIdType.MESH
NT_DIMS = (((1,), (1,)), ((), ()))


def bin_kernel(tile_ref, frames_ref, slot_ref, weight_ref, out_ref, *, blocks):
    step = pl.program_id(0)
    pos = frames_ref.shape[0]

    @pl.when(step == 0)
    def _():
        out_ref[...] = jnp.zeros_like(out_ref)

    row_id = lax.broadcasted_iota(jnp.int32, (TILE, TILE), 0).astype(jnp.bfloat16)
    zero = jnp.zeros((TILE, TILE), jnp.bfloat16)
    for pair in range(blocks // 2):
        parts = []
        for half in range(2):
            b = 2 * pair + half
            slot = jnp.broadcast_to(slot_ref[b : b + 1, :].astype(jnp.float32), (TILE, TILE))
            weight = jnp.broadcast_to(weight_ref[b : b + 1, :].astype(jnp.float32), (TILE, TILE))
            spread = jnp.where(slot.astype(jnp.bfloat16) == row_id, weight.astype(jnp.bfloat16), zero)
            parts.append(
                jnp.concatenate([spread, zero] if half == 0 else [zero, spread], axis=1)
            )
        spread = jnp.concatenate(parts, axis=0)
        both = lax.dot_general(
            frames_ref[:, 2 * pair * TILE : (2 * pair + 2) * TILE],
            spread,
            NT_DIMS,
            preferred_element_type=jnp.float32,
        )
        for half in range(2):
            t = tile_ref[step * blocks + 2 * pair + half]
            out_ref[t] += both[:, half * TILE : (half + 1) * TILE]


def bin_frames(frames, pixel_weight, pixel_slot, block_tile):
    pos, pixels = frames.shape
    chunk = min(CHUNK, pixels)
    blocks = chunk // TILE
    tiles = Q // TILE
    return pl.pallas_call(
        functools.partial(bin_kernel, blocks=blocks),
        grid_spec=pltpu.PrefetchScalarGridSpec(
            num_scalar_prefetch=1,
            grid=(pixels // chunk,),
            in_specs=[
                pl.BlockSpec((pos, chunk), lambda i, t: (0, i)),
                pl.BlockSpec((blocks, TILE), lambda i, t: (i, 0)),
                pl.BlockSpec((blocks, TILE), lambda i, t: (i, 0)),
            ],
            out_specs=pl.BlockSpec((tiles, pos, TILE), lambda i, t: (0, 0, 0)),
        ),
        out_shape=jax.ShapeDtypeStruct((tiles, pos, TILE), jnp.float32),
        compiler_params=pltpu.CompilerParams(vmem_limit_bytes=40 * 1024 * 1024),
        cost_estimate=pl.CostEstimate(
            flops=4 * pos * pixels * TILE, bytes_accessed=2 * pos * pixels, transcendentals=0
        ),
        name="bin_frames",
    )(
        block_tile,
        frames,
        pixel_slot.reshape(-1, TILE),
        pixel_weight.reshape(-1, TILE),
    )


def meet(left, right):
    return lax.dot_general(left, right, NT_DIMS, preferred_element_type=jnp.float32)


def count_pairs(ray_ref, pair_ref, start, stop):
    angles, rows, width = ray_ref.shape
    nt = pair_ref.shape[0] // angles

    def eight_rows(i, carry):
        row_id = lax.broadcasted_iota(jnp.int32, (nt, width), 0).astype(jnp.bfloat16)
        one = jnp.ones((nt, width), jnp.bfloat16)
        zero = jnp.zeros((nt, width), jnp.bfloat16)
        begin = pl.multiple_of(i * 8, 8)
        held = [ray_ref[a, pl.ds(begin, 8), :].astype(jnp.float32) for a in range(angles)]
        for r in range(8):
            hits = []
            for a in range(angles):
                index = jnp.broadcast_to(held[a][r : r + 1, :], (nt, width))
                hits.append(jnp.where(index.astype(jnp.bfloat16) == row_id, one, zero))
            first = jnp.concatenate(hits[:2], axis=0)
            last = jnp.concatenate(hits[2:], axis=0)
            pair_ref[: 2 * nt, 2 * nt :] += meet(first, last)
            pair_ref[:nt, : 2 * nt] += meet(hits[0], first)
            pair_ref[2 * nt : 3 * nt, 2 * nt :] += meet(hits[2], last)
        return carry

    lax.fori_loop(start, stop, eight_rows, 0)


def finish_pairs(pair_ref, high_ref, low_ref, count_ref, nt):
    same = lax.broadcasted_iota(jnp.int32, (nt, nt), 0) == lax.broadcasted_iota(jnp.int32, (nt, nt), 1)
    for base in (0, 2 * nt):
        block = pair_ref[base : base + nt, base : base + 2 * nt]
        held = jnp.sum(block, axis=0, keepdims=True)
        count_ref[:, base : base + 2 * nt] = jnp.broadcast_to(held, (8, 2 * nt))
        pair_ref[base + nt : base + 2 * nt, base : base + nt] = block[:, nt:].T
        pair_ref[base + nt : base + 2 * nt, base + nt : base + 2 * nt] = jnp.where(
            same, jnp.broadcast_to(held[:, nt:], (nt, nt)), 0.0
        )
    pair_ref[2 * nt :, : 2 * nt] = pair_ref[: 2 * nt, 2 * nt :].T
    value = pair_ref[...]
    high = jnp.floor(value * (1.0 / 256.0))
    high_ref[...] = high.astype(jnp.bfloat16)
    low_ref[...] = (value - 256.0 * high).astype(jnp.bfloat16)


def greet(peers):
    barrier = pltpu.get_barrier_semaphore()
    for peer in peers:
        pl.semaphore_signal(barrier, inc=1, device_id=peer, device_id_type=MESH)
    pl.semaphore_wait(barrier, len(peers))


def others(axis, size):
    me = lax.axis_index(axis)
    return [{axis: lax.rem(me + d, size)} for d in range(1, size)]


def swap(axis, size, send, land, send_sem, recv_sem):
    me = lax.axis_index(axis)
    copies = [
        pltpu.make_async_remote_copy(
            src_ref=send,
            dst_ref=land(me),
            send_sem=send_sem.at[d],
            recv_sem=recv_sem.at[d],
            device_id={axis: lax.rem(me + d, size)},
            device_id_type=MESH,
        )
        for d in range(1, size)
    ]
    for copy in copies:
        copy.start()
    return copies


def gather_kernel(
    own_ref, ray_ref, all_ref, high_ref, low_ref, count_ref, pair_ref, send_sem, recv_sem, *, scan, band, pix
):
    s, b, p = lax.axis_index("scan"), lax.axis_index("band"), lax.axis_index("pix")
    groups = ray_ref.shape[1] // 8
    cuts = [0, groups // 4, groups * 3 // 4, groups]
    greet(others("scan", scan) + others("band", band) + others("pix", pix))
    all_ref[p, b, s] = own_ref[...]
    copies = swap(
        "scan", scan, all_ref.at[p, b, s], lambda r: all_ref.at[p, b, r], send_sem.at[0], recv_sem.at[0]
    )
    pair_ref[...] = jnp.zeros_like(pair_ref)
    count_pairs(ray_ref, pair_ref, cuts[0], cuts[1])
    for copy in copies:
        copy.wait()
    copies = swap(
        "band", band, all_ref.at[p, b], lambda r: all_ref.at[p, r], send_sem.at[1], recv_sem.at[1]
    )
    count_pairs(ray_ref, pair_ref, cuts[1], cuts[2])
    for copy in copies:
        copy.wait()
    copies = swap("pix", pix, all_ref.at[p], lambda r: all_ref.at[r], send_sem.at[2], recv_sem.at[2])
    count_pairs(ray_ref, pair_ref, cuts[2], cuts[3])
    finish_pairs(pair_ref, high_ref, low_ref, count_ref, pair_ref.shape[0] // ray_ref.shape[0])
    for copy in copies:
        copy.wait()


def gather_spectra(spectra, rays, translations, scan, band, pix):
    comps, width = spectra.shape
    most = max(scan, band, pix)
    total = rays.shape[0] * translations
    vmem = pl.BlockSpec(memory_space=pltpu.VMEM)
    whole, high, low, counts = pl.pallas_call(
        functools.partial(gather_kernel, scan=scan, band=band, pix=pix),
        out_shape=[
            jax.ShapeDtypeStruct((pix, band, scan, comps, width), jnp.float32),
            jax.ShapeDtypeStruct((total, total), jnp.bfloat16),
            jax.ShapeDtypeStruct((total, total), jnp.bfloat16),
            jax.ShapeDtypeStruct((8, total), jnp.float32),
        ],
        in_specs=[vmem] * 2,
        out_specs=[vmem] * 4,
        scratch_shapes=[
            pltpu.VMEM((total, total), jnp.float32),
            pltpu.SemaphoreType.DMA((3, most)),
            pltpu.SemaphoreType.DMA((3, most)),
        ],
        compiler_params=pltpu.CompilerParams(
            collective_id=0, has_side_effects=True, vmem_limit_bytes=40 * 1024 * 1024
        ),
        name="gather_spectra",
    )(spectra, rays)
    spread = whole.transpose(3, 2, 1, 0, 4).reshape(comps, scan * band * pix * width)
    return spread, high, low, counts


def sirt_kernel(
    part_ref, high_ref, low_ref, count_ref, out_ref,
    group, place, count_pix, count_mid, count_scan, proj, proj_pix, proj_mid, proj_scan,
    send_sem, recv_sem, *, scan, band, pix, scale,
):
    s, b, p = lax.axis_index("scan"), lax.axis_index("band"), lax.axis_index("pix")
    sizes = band * pix
    rank = b * pix + p
    group_peers = []
    for d in range(1, sizes):
        peer = lax.rem(rank + d, sizes)
        group_peers.append({"band": lax.div(peer, pix), "pix": lax.rem(peer, pix)})
    greet(group_peers + others("scan", scan))

    copies = []
    for d, peer in zip(range(1, sizes), group_peers):
        copy = pltpu.make_async_remote_copy(
            src_ref=part_ref.at[peer["band"]],
            dst_ref=group.at[d],
            send_sem=send_sem.at[0, d],
            recv_sem=recv_sem.at[0, d],
            device_id=peer,
            device_id_type=MESH,
        )
        copy.start()
        copies.append(copy)
    copies += swap("pix", pix, count_ref, lambda r: count_pix.at[r], send_sem.at[1], recv_sem.at[1])
    count_pix[p] = count_ref[...]
    for copy in copies:
        copy.wait()
    value = part_ref[b]
    for d in range(1, sizes):
        value += group[d]
    place[s] = value
    counted = count_pix[0]
    for r in range(1, pix):
        counted += count_pix[r]
    count_mid[...] = counted
    count_scan[s] = counted
    copies = swap("scan", scan, place.at[s], lambda r: place.at[r], send_sem.at[2], recv_sem.at[2])
    copies += swap("scan", scan, count_mid, lambda r: count_scan.at[r], send_sem.at[3], recv_sem.at[3])
    for copy in copies:
        copy.wait()
    counted = count_scan[0]
    for r in range(1, scan):
        counted += count_scan[r]
    coefficients = jnp.concatenate([place[r] for r in range(scan)], axis=1)
    comps, rays = coefficients.shape
    ray_count = jnp.broadcast_to(counted[0:1], (comps, rays))
    total = coefficients / ray_count
    for k in range(ITERS - 1):
        lead = total.astype(jnp.bfloat16).astype(jnp.float32)
        rest = total - lead
        middle = rest.astype(jnp.bfloat16).astype(jnp.float32)
        pieces = jnp.concatenate([lead, middle, rest - middle], axis=0).astype(jnp.bfloat16)
        both = 256.0 * jnp.dot(pieces, high_ref[...], preferred_element_type=jnp.float32)
        both += jnp.dot(pieces, low_ref[...], preferred_element_type=jnp.float32)
        local = both[:comps] + (both[comps : 2 * comps] + both[2 * comps :])
        proj[k] = local
        proj_pix[k, p] = local
        for copy in swap(
            "pix", pix, proj.at[k], lambda r: proj_pix.at[k, r], send_sem.at[4 + 2 * k], recv_sem.at[4 + 2 * k]
        ):
            copy.wait()
        value = proj_pix[k, 0]
        for r in range(1, pix):
            value += proj_pix[k, r]
        proj_mid[k] = value
        proj_scan[k, s] = value
        for copy in swap(
            "scan", scan, proj_mid.at[k], lambda r: proj_scan.at[k, r], send_sem.at[5 + 2 * k], recv_sem.at[5 + 2 * k]
        ):
            copy.wait()
        value = proj_scan[k, 0]
        for r in range(1, scan):
            value += proj_scan[k, r]
        total += (coefficients - scale * value) / ray_count
    out_ref[...] = total


def sirt_table(parts, high, low, counts, scan, pix, scale):
    band, comps, pos = parts.shape
    rays = high.shape[0]
    most = max(scan, band * pix)
    steps = ITERS - 1
    vmem = pl.BlockSpec(memory_space=pltpu.VMEM)
    f32 = jnp.float32
    return pl.pallas_call(
        functools.partial(sirt_kernel, scan=scan, band=band, pix=pix, scale=scale),
        out_shape=jax.ShapeDtypeStruct((comps, rays), f32),
        in_specs=[vmem] * 4,
        out_specs=vmem,
        scratch_shapes=[
            pltpu.VMEM((band * pix, comps, pos), f32),
            pltpu.VMEM((scan, comps, pos), f32),
            pltpu.VMEM((pix, 8, rays), f32),
            pltpu.VMEM((8, rays), f32),
            pltpu.VMEM((scan, 8, rays), f32),
            pltpu.VMEM((steps, comps, rays), f32),
            pltpu.VMEM((steps, pix, comps, rays), f32),
            pltpu.VMEM((steps, comps, rays), f32),
            pltpu.VMEM((steps, scan, comps, rays), f32),
            pltpu.SemaphoreType.DMA((4 + 2 * steps, most)),
            pltpu.SemaphoreType.DMA((4 + 2 * steps, most)),
        ],
        compiler_params=pltpu.CompilerParams(
            collective_id=1, has_side_effects=True, vmem_limit_bytes=40 * 1024 * 1024
        ),
        name="sirt_table",
    )(parts, high, low, counts)


def back_kernel(table_ref, ray_ref, out_ref, *, translations):
    comps, rows, width = out_ref.shape
    angles = ray_ref.shape[0]

    def eight_rows(i, carry):
        begin = pl.multiple_of(i * 8, 8)
        for w in range(0, width, translations):
            values = [None] * comps
            for a in range(angles):
                index = ray_ref[a, pl.ds(begin, 8), w : w + translations]
                for c in range(comps):
                    table = jnp.broadcast_to(table_ref[c, a : a + 1, :], (8, translations))
                    got = jnp.take_along_axis(table, index, axis=1, mode="promise_in_bounds")
                    values[c] = got if a == 0 else values[c] + got
            for c in range(comps):
                out_ref[c, pl.ds(begin, 8), w : w + translations] = values[c]
        return carry

    lax.fori_loop(0, rows // 8, eight_rows, 0)


def back_project(table, rays, translations):
    comps = table.shape[0]
    angles, rows, width = rays.shape
    group = min(8, comps)
    return pl.pallas_call(
        functools.partial(back_kernel, translations=translations),
        grid=(comps // group,),
        in_specs=[
            pl.BlockSpec((group, angles, translations), lambda i: (i, 0, 0)),
            pl.BlockSpec((angles, rows, width), lambda i: (0, 0, 0)),
        ],
        out_specs=pl.BlockSpec((group, rows, width), lambda i: (i, 0, 0)),
        out_shape=jax.ShapeDtypeStruct((comps, rows, width), jnp.float32),
        compiler_params=pltpu.CompilerParams(vmem_limit_bytes=40 * 1024 * 1024),
        cost_estimate=pl.CostEstimate(
            flops=comps * angles * rows * width, bytes_accessed=4 * comps * rows * width, transcendentals=0
        ),
        name="back_project",
    )(table.reshape(comps, angles, translations), rays)


def shards(frames, pixel_weight, pixel_slot, block_tile, spectra, ray_index):
    highest = lax.Precision.HIGHEST
    scan_count = lax.axis_size("scan")
    band_count = lax.axis_size("band")
    pos_local, pix_local = frames.shape
    comp_total, bin_local = spectra.shape
    angles, row_local, img_width = ray_index.shape
    pos_total = pos_local * scan_count
    translations = pos_total // angles
    comp_local = comp_total // band_count

    pix_count = lax.axis_size("pix")
    all_spectra, high, low, counts = gather_spectra(
        spectra, ray_index, translations, scan_count, band_count, pix_count
    )
    bins = bin_frames(frames, pixel_weight, pixel_slot, block_tile)
    gram = lax.dot_general(all_spectra, all_spectra, NT_DIMS, precision=highest)
    factor = jnp.linalg.cholesky(gram)
    moments_part = jnp.einsum(
        "ctl,tpl->cp", all_spectra.reshape(comp_total, Q // TILE, TILE), bins, precision=highest
    )
    parts = jax.scipy.linalg.cho_solve((factor, True), moments_part)
    parts = parts.reshape(band_count, comp_local, pos_local)
    total = sirt_table(parts, high, low, counts, scan_count, pix_count, RELAX / angles)
    return back_project((RELAX * img_width / angles) * total, ray_index, translations)


def solution(mesh):
    return jax.shard_map(
        shards,
        mesh=mesh,
        in_specs=(
            P(("slices", "scan"), ("band", "pix")),
            P(("band", "pix")),
            P(("band", "pix")),
            P(("band", "pix")),
            P(None, ("scan", "band", "pix")),
            P(None, ("scan", "pix"), None),
        ),
        out_specs=P(("slices", "band"), ("scan", "pix"), None),
        check_vma=False,
    )
```

```python
import functools

import jax
import jax.numpy as jnp
from jax import lax
from jax.experimental import pallas as pl
from jax.experimental.pallas import tpu as pltpu
from jax.sharding import PartitionSpec as P

TILE = 128
Q = 2048
ITERS = 3
RELAX = 1.5
CHUNK = 16384
MESH = pl.DeviceIdType.MESH
NT_DIMS = (((1,), (1,)), ((), ()))


def bin_kernel(tile_ref, frames_ref, slot_ref, weight_ref, out_ref, *, blocks):
    step = pl.program_id(0)
    pos = frames_ref.shape[0]

    @pl.when(step == 0)
    def _():
        out_ref[...] = jnp.zeros_like(out_ref)

    row_id = lax.broadcasted_iota(jnp.int32, (TILE, TILE), 0).astype(jnp.bfloat16)
    zero = jnp.zeros((TILE, TILE), jnp.bfloat16)
    for pair in range(blocks // 2):
        parts = []
        for half in range(2):
            b = 2 * pair + half
            slot = jnp.broadcast_to(slot_ref[b : b + 1, :].astype(jnp.float32), (TILE, TILE))
            weight = jnp.broadcast_to(weight_ref[b : b + 1, :].astype(jnp.float32), (TILE, TILE))
            spread = jnp.where(slot.astype(jnp.bfloat16) == row_id, weight.astype(jnp.bfloat16), zero)
            parts.append(
                jnp.concatenate([spread, zero] if half == 0 else [zero, spread], axis=1)
            )
        spread = jnp.concatenate(parts, axis=0)
        both = lax.dot_general(
            frames_ref[:, 2 * pair * TILE : (2 * pair + 2) * TILE],
            spread,
            NT_DIMS,
            preferred_element_type=jnp.float32,
        )
        for half in range(2):
            t = tile_ref[step * blocks + 2 * pair + half]
            out_ref[t] += both[:, half * TILE : (half + 1) * TILE]


def bin_frames(frames, pixel_weight, pixel_slot, block_tile):
    pos, pixels = frames.shape
    chunk = min(CHUNK, pixels)
    blocks = chunk // TILE
    tiles = Q // TILE
    return pl.pallas_call(
        functools.partial(bin_kernel, blocks=blocks),
        grid_spec=pltpu.PrefetchScalarGridSpec(
            num_scalar_prefetch=1,
            grid=(pixels // chunk,),
            in_specs=[
                pl.BlockSpec((pos, chunk), lambda i, t: (0, i)),
                pl.BlockSpec((blocks, TILE), lambda i, t: (i, 0)),
                pl.BlockSpec((blocks, TILE), lambda i, t: (i, 0)),
            ],
            out_specs=pl.BlockSpec((tiles, pos, TILE), lambda i, t: (0, 0, 0)),
        ),
        out_shape=jax.ShapeDtypeStruct((tiles, pos, TILE), jnp.float32),
        compiler_params=pltpu.CompilerParams(vmem_limit_bytes=40 * 1024 * 1024),
        cost_estimate=pl.CostEstimate(
            flops=4 * pos * pixels * TILE, bytes_accessed=2 * pos * pixels, transcendentals=0
        ),
        name="bin_frames",
    )(
        block_tile,
        frames,
        pixel_slot.reshape(-1, TILE),
        pixel_weight.reshape(-1, TILE),
    )


def meet(left, right):
    return lax.dot_general(left, right, NT_DIMS, preferred_element_type=jnp.float32)


def count_pairs(ray_ref, pair_ref, start, stop):
    angles, rows, width = ray_ref.shape
    nt = pair_ref.shape[0] // angles

    def eight_rows(i, carry):
        row_id = lax.broadcasted_iota(jnp.int32, (nt, width), 0).astype(jnp.bfloat16)
        one = jnp.ones((nt, width), jnp.bfloat16)
        zero = jnp.zeros((nt, width), jnp.bfloat16)
        begin = pl.multiple_of(i * 8, 8)
        held = [ray_ref[a, pl.ds(begin, 8), :].astype(jnp.float32) for a in range(angles)]
        for r in range(8):
            hits = []
            for a in range(angles):
                index = jnp.broadcast_to(held[a][r : r + 1, :], (nt, width))
                hits.append(jnp.where(index.astype(jnp.bfloat16) == row_id, one, zero))
            first = jnp.concatenate(hits[:2], axis=0)
            last = jnp.concatenate(hits[2:], axis=0)
            pair_ref[: 2 * nt, 2 * nt :] += meet(first, last)
            pair_ref[:nt, : 2 * nt] += meet(hits[0], first)
            pair_ref[2 * nt : 3 * nt, 2 * nt :] += meet(hits[2], last)
        return carry

    lax.fori_loop(start, stop, eight_rows, 0)


def finish_pairs(pair_ref, high_ref, low_ref, count_ref, nt):
    same = lax.broadcasted_iota(jnp.int32, (nt, nt), 0) == lax.broadcasted_iota(jnp.int32, (nt, nt), 1)
    for base in (0, 2 * nt):
        block = pair_ref[base : base + nt, base : base + 2 * nt]
        held = jnp.sum(block, axis=0, keepdims=True)
        count_ref[:, base : base + 2 * nt] = jnp.broadcast_to(held, (8, 2 * nt))
        pair_ref[base + nt : base + 2 * nt, base : base + nt] = block[:, nt:].T
        pair_ref[base + nt : base + 2 * nt, base + nt : base + 2 * nt] = jnp.where(
            same, jnp.broadcast_to(held[:, nt:], (nt, nt)), 0.0
        )
    pair_ref[2 * nt :, : 2 * nt] = pair_ref[: 2 * nt, 2 * nt :].T
    value = pair_ref[...]
    high = jnp.floor(value * (1.0 / 256.0))
    high_ref[...] = high.astype(jnp.bfloat16)
    low_ref[...] = (value - 256.0 * high).astype(jnp.bfloat16)


def greet(peers):
    barrier = pltpu.get_barrier_semaphore()
    for peer in peers:
        pl.semaphore_signal(barrier, inc=1, device_id=peer, device_id_type=MESH)
    pl.semaphore_wait(barrier, len(peers))


def others(axis, size):
    me = lax.axis_index(axis)
    return [{axis: lax.rem(me + d, size)} for d in range(1, size)]


def swap(axis, size, send, land, send_sem, recv_sem):
    me = lax.axis_index(axis)
    copies = [
        pltpu.make_async_remote_copy(
            src_ref=send,
            dst_ref=land(me),
            send_sem=send_sem.at[d],
            recv_sem=recv_sem.at[d],
            device_id={axis: lax.rem(me + d, size)},
            device_id_type=MESH,
        )
        for d in range(1, size)
    ]
    for copy in copies:
        copy.start()
    return copies


def gather_kernel(
    own_ref, ray_ref, all_ref, high_ref, low_ref, count_ref, pair_ref, send_sem, recv_sem, *, scan, band, pix
):
    s, b, p = lax.axis_index("scan"), lax.axis_index("band"), lax.axis_index("pix")
    groups = ray_ref.shape[1] // 8
    cuts = [0, groups // 4, groups * 3 // 4, groups]
    greet(others("scan", scan) + others("band", band) + others("pix", pix))
    all_ref[p, b, s] = own_ref[...]
    copies = swap(
        "scan", scan, all_ref.at[p, b, s], lambda r: all_ref.at[p, b, r], send_sem.at[0], recv_sem.at[0]
    )
    pair_ref[...] = jnp.zeros_like(pair_ref)
    count_pairs(ray_ref, pair_ref, cuts[0], cuts[1])
    for copy in copies:
        copy.wait()
    copies = swap(
        "band", band, all_ref.at[p, b], lambda r: all_ref.at[p, r], send_sem.at[1], recv_sem.at[1]
    )
    count_pairs(ray_ref, pair_ref, cuts[1], cuts[2])
    for copy in copies:
        copy.wait()
    copies = swap("pix", pix, all_ref.at[p], lambda r: all_ref.at[r], send_sem.at[2], recv_sem.at[2])
    count_pairs(ray_ref, pair_ref, cuts[2], cuts[3])
    finish_pairs(pair_ref, high_ref, low_ref, count_ref, pair_ref.shape[0] // ray_ref.shape[0])
    for copy in copies:
        copy.wait()


def gather_spectra(spectra, rays, translations, scan, band, pix):
    comps, width = spectra.shape
    most = max(scan, band, pix)
    total = rays.shape[0] * translations
    vmem = pl.BlockSpec(memory_space=pltpu.VMEM)
    whole, high, low, counts = pl.pallas_call(
        functools.partial(gather_kernel, scan=scan, band=band, pix=pix),
        out_shape=[
            jax.ShapeDtypeStruct((pix, band, scan, comps, width), jnp.float32),
            jax.ShapeDtypeStruct((total, total), jnp.bfloat16),
            jax.ShapeDtypeStruct((total, total), jnp.bfloat16),
            jax.ShapeDtypeStruct((8, total), jnp.float32),
        ],
        in_specs=[vmem] * 2,
        out_specs=[vmem] * 4,
        scratch_shapes=[
            pltpu.VMEM((total, total), jnp.float32),
            pltpu.SemaphoreType.DMA((3, most)),
            pltpu.SemaphoreType.DMA((3, most)),
        ],
        compiler_params=pltpu.CompilerParams(
            collective_id=0, has_side_effects=True, vmem_limit_bytes=40 * 1024 * 1024
        ),
        name="gather_spectra",
    )(spectra, rays)
    spread = whole.transpose(3, 2, 1, 0, 4).reshape(comps, scan * band * pix * width)
    return spread, high, low, counts


def sirt_kernel(
    part_ref, high_ref, low_ref, count_ref, out_ref,
    group, place, count_pix, count_mid, count_scan, proj, proj_pix, proj_mid, proj_scan,
    send_sem, recv_sem, *, scan, band, pix, scale,
):
    s, b, p = lax.axis_index("scan"), lax.axis_index("band"), lax.axis_index("pix")
    sizes = band * pix
    rank = b * pix + p
    group_peers = []
    for d in range(1, sizes):
        peer = lax.rem(rank + d, sizes)
        group_peers.append({"band": lax.div(peer, pix), "pix": lax.rem(peer, pix)})
    greet(group_peers + others("scan", scan))

    copies = []
    for d, peer in zip(range(1, sizes), group_peers):
        copy = pltpu.make_async_remote_copy(
            src_ref=part_ref.at[peer["band"]],
            dst_ref=group.at[d],
            send_sem=send_sem.at[0, d],
            recv_sem=recv_sem.at[0, d],
            device_id=peer,
            device_id_type=MESH,
        )
        copy.start()
        copies.append(copy)
    copies += swap("pix", pix, count_ref, lambda r: count_pix.at[r], send_sem.at[1], recv_sem.at[1])
    count_pix[p] = count_ref[...]
    for copy in copies:
        copy.wait()
    value = part_ref[b]
    for d in range(1, sizes):
        value += group[d]
    place[s] = value
    counted = count_pix[0]
    for r in range(1, pix):
        counted += count_pix[r]
    count_mid[...] = counted
    count_scan[s] = counted
    copies = swap("scan", scan, place.at[s], lambda r: place.at[r], send_sem.at[2], recv_sem.at[2])
    copies += swap("scan", scan, count_mid, lambda r: count_scan.at[r], send_sem.at[3], recv_sem.at[3])
    for copy in copies:
        copy.wait()
    counted = count_scan[0]
    for r in range(1, scan):
        counted += count_scan[r]
    coefficients = jnp.concatenate([place[r] for r in range(scan)], axis=1)
    comps, rays = coefficients.shape
    ray_count = jnp.broadcast_to(counted[0:1], (comps, rays))
    total = coefficients / ray_count
    for k in range(ITERS - 1):
        lead = total.astype(jnp.bfloat16).astype(jnp.float32)
        rest = total - lead
        middle = rest.astype(jnp.bfloat16).astype(jnp.float32)
        pieces = jnp.concatenate([lead, middle, rest - middle], axis=0).astype(jnp.bfloat16)
        both = 256.0 * jnp.dot(pieces, high_ref[...], preferred_element_type=jnp.float32)
        both += jnp.dot(pieces, low_ref[...], preferred_element_type=jnp.float32)
        local = both[:comps] + (both[comps : 2 * comps] + both[2 * comps :])
        proj[k] = local
        proj_pix[k, p] = local
        for copy in swap(
            "pix", pix, proj.at[k], lambda r: proj_pix.at[k, r], send_sem.at[4 + 2 * k], recv_sem.at[4 + 2 * k]
        ):
            copy.wait()
        value = proj_pix[k, 0]
        for r in range(1, pix):
            value += proj_pix[k, r]
        proj_mid[k] = value
        proj_scan[k, s] = value
        for copy in swap(
            "scan", scan, proj_mid.at[k], lambda r: proj_scan.at[k, r], send_sem.at[5 + 2 * k], recv_sem.at[5 + 2 * k]
        ):
            copy.wait()
        value = proj_scan[k, 0]
        for r in range(1, scan):
            value += proj_scan[k, r]
        total += (coefficients - scale * value) / ray_count
    out_ref[...] = total


def sirt_table(parts, high, low, counts, scan, pix, scale):
    band, comps, pos = parts.shape
    rays = high.shape[0]
    most = max(scan, band * pix)
    steps = ITERS - 1
    vmem = pl.BlockSpec(memory_space=pltpu.VMEM)
    f32 = jnp.float32
    return pl.pallas_call(
        functools.partial(sirt_kernel, scan=scan, band=band, pix=pix, scale=scale),
        out_shape=jax.ShapeDtypeStruct((comps, rays), f32),
        in_specs=[vmem] * 4,
        out_specs=vmem,
        scratch_shapes=[
            pltpu.VMEM((band * pix, comps, pos), f32),
            pltpu.VMEM((scan, comps, pos), f32),
            pltpu.VMEM((pix, 8, rays), f32),
            pltpu.VMEM((8, rays), f32),
            pltpu.VMEM((scan, 8, rays), f32),
            pltpu.VMEM((steps, comps, rays), f32),
            pltpu.VMEM((steps, pix, comps, rays), f32),
            pltpu.VMEM((steps, comps, rays), f32),
            pltpu.VMEM((steps, scan, comps, rays), f32),
            pltpu.SemaphoreType.DMA((4 + 2 * steps, most)),
            pltpu.SemaphoreType.DMA((4 + 2 * steps, most)),
        ],
        compiler_params=pltpu.CompilerParams(
            collective_id=1, has_side_effects=True, vmem_limit_bytes=40 * 1024 * 1024
        ),
        name="sirt_table",
    )(parts, high, low, counts)


def back_kernel(table_ref, ray_ref, out_ref, *, translations):
    comps, rows, width = out_ref.shape
    angles = ray_ref.shape[0]

    def eight_rows(i, carry):
        begin = pl.multiple_of(i * 8, 8)
        for w in range(0, width, translations):
            values = [None] * comps
            for a in range(angles):
                index = ray_ref[a, pl.ds(begin, 8), w : w + translations]
                for c in range(comps):
                    table = jnp.broadcast_to(table_ref[c, a : a + 1, :], (8, translations))
                    got = jnp.take_along_axis(table, index, axis=1, mode="promise_in_bounds")
                    values[c] = got if a == 0 else values[c] + got
            for c in range(comps):
                out_ref[c, pl.ds(begin, 8), w : w + translations] = values[c]
        return carry

    lax.fori_loop(0, rows // 8, eight_rows, 0)


def back_project(table, rays, translations):
    comps = table.shape[0]
    angles, rows, width = rays.shape
    group = min(8, comps)
    return pl.pallas_call(
        functools.partial(back_kernel, translations=translations),
        grid=(comps // group,),
        in_specs=[
            pl.BlockSpec((group, angles, translations), lambda i: (i, 0, 0)),
            pl.BlockSpec((angles, rows, width), lambda i: (0, 0, 0)),
        ],
        out_specs=pl.BlockSpec((group, rows, width), lambda i: (i, 0, 0)),
        out_shape=jax.ShapeDtypeStruct((comps, rows, width), jnp.float32),
        compiler_params=pltpu.CompilerParams(vmem_limit_bytes=40 * 1024 * 1024),
        cost_estimate=pl.CostEstimate(
            flops=comps * angles * rows * width, bytes_accessed=4 * comps * rows * width, transcendentals=0
        ),
        name="back_project",
    )(table.reshape(comps, angles, translations), rays)


def shards(frames, pixel_weight, pixel_slot, block_tile, spectra, ray_index):
    highest = lax.Precision.HIGHEST
    scan_count = lax.axis_size("scan")
    band_count = lax.axis_size("band")
    pos_local, pix_local = frames.shape
    comp_total, bin_local = spectra.shape
    angles, row_local, img_width = ray_index.shape
    pos_total = pos_local * scan_count
    translations = pos_total // angles
    comp_local = comp_total // band_count

    pix_count = lax.axis_size("pix")
    all_spectra, high, low, counts = gather_spectra(
        spectra, ray_index, translations, scan_count, band_count, pix_count
    )
    bins = bin_frames(frames, pixel_weight, pixel_slot, block_tile)
    gram = lax.dot_general(all_spectra, all_spectra, NT_DIMS, precision=highest)
    factor = jnp.linalg.cholesky(gram)
    moments_part = jnp.einsum(
        "ctl,tpl->cp", all_spectra.reshape(comp_total, Q // TILE, TILE), bins, precision=highest
    )
    parts = jax.scipy.linalg.cho_solve((factor, True), moments_part)
    parts = parts.reshape(band_count, comp_local, pos_local)
    total = sirt_table(parts, high, low, counts, scan_count, pix_count, RELAX / angles)
    return back_project((RELAX * img_width / angles) * total, ray_index, translations)


def solution(mesh):
    return jax.shard_map(
        shards,
        mesh=mesh,
        in_specs=(
            P(("slices", "scan"), ("band", "pix")),
            P(("band", "pix")),
            P(("band", "pix")),
            P(("band", "pix")),
            P(None, ("scan", "band", "pix")),
            P(None, ("scan", "pix"), None),
        ),
        out_specs=P(("slices", "band"), ("scan", "pix"), None),
        check_vma=False,
    )
```
